256 devices in a mesh: ctx: 256 (over y, z, x, core).
Axes of the slice: x: 4, y: 4, z: 8, core: 2. Of those that a mesh axis runs over, the one named last changes fastest.
Arguments:
- queries: bfloat16 [131072, 2048], P('ctx'), may hold values from -26 to 26
- attention_key_rows: bfloat16 [131072, 256], P('ctx'), may hold values from -4 to 4
- attention_value_rows: bfloat16 [131072, 256], P('ctx'), may hold values from -6 to 6
- output_gradient: bfloat16 [131072, 2048], P('ctx'), may hold values from -6 to 6
- parent_block: int32 [1024], replicated, may hold values from -1 to 1022, as said below
- seg_start: int32 [1024], replicated, may hold values from 0 to 127
Outputs:
- grad_queries: bfloat16 [131072, 2048], P('ctx')
- key_gradient_rows: bfloat16 [131072, 256], P('ctx')
- value_gradient_rows: bfloat16 [131072, 256], P('ctx')
The draws below stay inside these ranges and needn't reach their ends.
Inputs may be any that keep to these rules, and one draw needn't show every extreme that they name: parent_block[g] is -1 or an earlier block lying on the same shard or on one of the 3 shards before it: parent_block[g] // 4 >= g // 4 - 3; that farthest distance is used in every draw.
All inputs are finite; a program needn't handle non-finite values.
Results may differ from the reference program's by a relative error of at most 0.007.
Values may be sent and summed in bfloat16 or wider, within the bound.
A program may use at most 64 MiB of HBM per device.

```python
import jax
import jax.numpy as jnp
from jax import lax

QUERY_HEADS = 32
KEY_VALUE_HEADS = 4
HEAD_SIZE = 64
BLOCK_TOKENS = 128
PARENT_SHARDS = 4
BLOCKS_DEV = 4
TOKEN_COUNT = 131072
BLOCK_COUNT = 1024


def shared_keys(key):
    unmasked_keys = jax.random.truncated_normal(jax.random.fold_in(key, 41), -4.0, 4.0, (TOKEN_COUNT, KEY_VALUE_HEADS, HEAD_SIZE), jnp.float32)
    return unmasked_keys


def draw_attention_key_rows(key, part):
    unmasked_keys = shared_keys(key)
    backward_result = unmasked_keys
    return backward_result.reshape(TOKEN_COUNT, KEY_VALUE_HEADS * HEAD_SIZE).astype(jnp.bfloat16)


def draw_queries(key, part):
    key = jax.random.fold_in(key, 5)
    drawn_rows = jax.random.truncated_normal(key, -4.0, 4.0, (TOKEN_COUNT, QUERY_HEADS, HEAD_SIZE), jnp.float32)
    backward_result = drawn_rows
    return backward_result.reshape(TOKEN_COUNT, QUERY_HEADS * HEAD_SIZE).astype(jnp.bfloat16)


def draw_parent_block(key, part):
    key = jax.random.fold_in(key, 11)
    block_ids = jnp.arange(BLOCK_COUNT, dtype=jnp.int32)
    device = block_ids // BLOCKS_DEV
    lowest = jnp.maximum(device - (PARENT_SHARDS - 1), 0) * BLOCKS_DEV
    block_kind = jax.random.randint(jax.random.fold_in(key, 1), (BLOCK_COUNT,), 0, 8)
    forked = jax.random.randint(jax.random.fold_in(key, 2), (BLOCK_COUNT,), lowest, jnp.maximum(block_ids, lowest + 1))
    chosen = jnp.where(block_kind == 0, -1, jnp.where(block_kind <= 3, forked, block_ids - 1))
    farthest = (block_ids % BLOCKS_DEV == 0) & (device >= PARENT_SHARDS - 1) & (device % 4 == 3)
    chosen = jnp.where(farthest, (device - (PARENT_SHARDS - 1)) * BLOCKS_DEV, chosen)
    chosen = jnp.where(block_ids == 0, -1, chosen)
    chosen = jnp.where(block_ids == BLOCK_COUNT - 1, BLOCK_COUNT - 2, chosen)
    return chosen.astype(jnp.int32)


def draw_seg_start(key, part):
    key = jax.random.fold_in(key, 13)
    block_ids = jnp.arange(BLOCK_COUNT, dtype=jnp.int32)
    offset = jax.random.randint(jax.random.fold_in(key, 1), (BLOCK_COUNT,), 1, BLOCK_TOKENS)
    begins = jax.random.randint(jax.random.fold_in(key, 2), (BLOCK_COUNT,), 0, 4) == 0
    chosen = jnp.where(begins, offset, 0)
    chosen = jnp.where(block_ids == 1, BLOCK_TOKENS - 1, chosen)
    return chosen.astype(jnp.int32)


def steps_of(rng, shape, shards, low, high):
    gain, own = 1.0, jax.random.fold_in(rng, 6)
    for axis_at, blocks in shards:
        heights = jnp.exp(jax.random.uniform(jax.random.fold_in(own, axis_at), (blocks,), jnp.float32, low / len(shards), high / len(shards)))
        gain = gain * jnp.repeat(heights, shape[axis_at] // blocks).reshape([-1 if axis == axis_at else 1 for axis in range(len(shape))])
    return gain


def normal_values(stream_key, dims, width, bound, pieces=(), kind=jnp.bfloat16):
    values = width * jax.random.normal(stream_key, dims, jnp.float32)
    if pieces:
        values = values * steps_of(stream_key, dims, pieces, -0.22, 0.18)
    return jnp.clip(values, -bound, bound).astype(kind)


def setup_inputs(seed: int = 0) -> dict:
    key_list = jax.random.split(jax.random.key(seed), 7)
    queries = draw_queries(jax.random.fold_in(key_list[6], 71), 0)
    attention_key_rows = draw_attention_key_rows(jax.random.fold_in(key_list[6], 71), 0)
    attention_value_rows = normal_values(key_list[2], (TOKEN_COUNT, KEY_VALUE_HEADS * HEAD_SIZE), 1.0, 6.0, ((0, 256),))
    output_gradient = normal_values(key_list[3], (TOKEN_COUNT, QUERY_HEADS * HEAD_SIZE), 1.0, 6.0, ((0, 256),))
    parent_block = draw_parent_block(jax.random.fold_in(key_list[6], 71), 0)
    seg_start = draw_seg_start(jax.random.fold_in(key_list[6], 71), 0)
    return {"queries": queries, "attention_key_rows": attention_key_rows, "attention_value_rows": attention_value_rows, "output_gradient": output_gradient, "parent_block": parent_block, "seg_start": seg_start}


NEG_FILL = -1e30


def block_mask(parent_id, own_start, parent_start):
    query_pos = jnp.arange(BLOCK_TOKENS)[:, None]
    key_pos = jnp.arange(BLOCK_TOKENS)[None, :]
    own_keys = (key_pos <= query_pos) & ((key_pos >= own_start) == (query_pos >= own_start))
    carried = (query_pos < own_start) | (own_start == 0)
    far_keys = (parent_id >= 0) & carried & (key_pos > query_pos) & (key_pos >= parent_start)
    return jnp.concatenate([far_keys, own_keys], axis=1)


def block_grads(query_block, keys_cat, values_cat, grad_block, key_mask):
    score_scale = HEAD_SIZE ** -0.5
    highest = lax.Precision.HIGHEST
    query_wide = query_block.astype(jnp.float32)
    grad_wide = grad_block.astype(jnp.float32)
    keys_wide = keys_cat.astype(jnp.float32)
    values_wide = values_cat.astype(jnp.float32)
    scores = jnp.einsum('ihgd,jhd->hgij', query_wide, keys_wide, precision=highest) * score_scale
    masked = jnp.where(key_mask[None, None], scores, NEG_FILL)
    row_max = jnp.max(masked, axis=-1, keepdims=True)
    weight = jnp.exp(masked - row_max)
    attn_prob = weight / jnp.sum(weight, axis=-1, keepdims=True)
    prob_low = lax.optimization_barrier(attn_prob.astype(jnp.bfloat16)).astype(jnp.float32)
    output = jnp.einsum('hgij,jhd->ihgd', prob_low, values_wide, precision=highest).astype(jnp.bfloat16)
    output = lax.optimization_barrier(output)
    row_delta = jnp.sum(grad_wide * output.astype(jnp.float32), axis=-1)
    grad_prob = jnp.einsum('ihgd,jhd->hgij', grad_wide, values_wide, precision=highest)
    grad_score = attn_prob * (grad_prob - jnp.transpose(row_delta, (1, 2, 0))[..., None])
    score_low = lax.optimization_barrier(grad_score.astype(jnp.bfloat16)).astype(jnp.float32)
    grad_query = jnp.einsum('hgij,jhd->ihgd', score_low, keys_wide, precision=highest) * score_scale
    grad_key = jnp.einsum('hgij,ihgd->jhd', score_low, query_wide, precision=highest) * score_scale
    grad_value = jnp.einsum('hgij,ihgd->jhd', prob_low, grad_wide, precision=highest)
    return grad_query, grad_key, grad_value


def reference(queries, attention_key_rows, attention_value_rows, output_gradient, parent_block, seg_start):
    head_groups = QUERY_HEADS // KEY_VALUE_HEADS
    blocked_queries = queries.reshape(BLOCK_COUNT, BLOCK_TOKENS, KEY_VALUE_HEADS, head_groups, HEAD_SIZE)
    gradient_blocks = output_gradient.reshape(BLOCK_COUNT, BLOCK_TOKENS, KEY_VALUE_HEADS, head_groups, HEAD_SIZE)
    blocked_keys = attention_key_rows.reshape(BLOCK_COUNT, BLOCK_TOKENS, KEY_VALUE_HEADS, HEAD_SIZE)
    blocked_values = attention_value_rows.reshape(BLOCK_COUNT, BLOCK_TOKENS, KEY_VALUE_HEADS, HEAD_SIZE)
    safe_parent = jnp.maximum(parent_block, 0)
    parent_start = seg_start[safe_parent]

    def one_block(inputs):
        query_block, grad_block, block_id, parent_id, own_start, far_start = inputs
        parent_safe = jnp.maximum(parent_id, 0)
        keys_cat = jnp.concatenate([blocked_keys[parent_safe], blocked_keys[block_id]], axis=0)
        values_cat = jnp.concatenate([blocked_values[parent_safe], blocked_values[block_id]], axis=0)
        key_mask = block_mask(parent_id, own_start, far_start)
        grad_query, grad_key, grad_value = block_grads(query_block, keys_cat, values_cat, grad_block, key_mask)
        return (grad_query.astype(jnp.bfloat16), grad_key[:BLOCK_TOKENS], grad_key[BLOCK_TOKENS:],
                grad_value[:BLOCK_TOKENS], grad_value[BLOCK_TOKENS:])

    block_ids = jnp.arange(BLOCK_COUNT).astype(jnp.int32)
    query_grad, far_key, own_key, far_value, own_value = lax.map(
        one_block, (blocked_queries, gradient_blocks, block_ids, parent_block, seg_start, parent_start))
    target = jnp.where(parent_block >= 0, parent_block, BLOCK_COUNT)
    key_gradient_sum = own_key + jax.ops.segment_sum(far_key, target, num_segments=BLOCK_COUNT + 1)[:BLOCK_COUNT]
    value_gradient_sum = own_value + jax.ops.segment_sum(far_value, target, num_segments=BLOCK_COUNT + 1)[:BLOCK_COUNT]
    grad_queries = query_grad.reshape(TOKEN_COUNT, QUERY_HEADS * HEAD_SIZE)
    key_gradient_rows = key_gradient_sum.reshape(TOKEN_COUNT, KEY_VALUE_HEADS * HEAD_SIZE).astype(jnp.bfloat16)
    value_gradient_rows = value_gradient_sum.reshape(TOKEN_COUNT, KEY_VALUE_HEADS * HEAD_SIZE).astype(jnp.bfloat16)
    return (grad_queries, key_gradient_rows, value_gradient_rows)
```

```python
import jax
import jax.numpy as jnp
from jax import lax
from jax.experimental import pallas as pl
from jax.experimental.pallas import tpu as pltpu
from jax.sharding import PartitionSpec as P

HEADS = 4
BLOCK = 128
BLOCKS = 4
ROWS = BLOCK * BLOCKS
F32, BF16 = jnp.float32, jnp.bfloat16
SCALE = 0.125
EXP2_SCALE = SCALE * 1.4426950408889634
NT = (((1,), (1,)), ((), ()))
NN = (((1,), (0,)), ((), ()))
TN = (((0,), (0,)), ((), ()))
MESH = pl.DeviceIdType.MESH


def dot(a, b, dims):
    return lax.dot_general(a, b, dims, preferred_element_type=F32)


def iota(shape, dim):
    return lax.broadcasted_iota(jnp.int32, shape, dim)


def swap_halves(x):
    return jnp.concatenate([x[:, 64:], x[:, :64]], 1)


def compute_block(h, b, own_kv, far_kv, q_ref, o_ref, dq_ref, bias_ref, own_ref, far_ref):
    rows = pl.ds(pl.multiple_of(b * BLOCK, BLOCK), BLOCK)
    kv = jnp.concatenate([own_kv, far_kv], 0)
    vk = swap_halves(kv)
    low = iota((256, 128), 1) < 64
    zero = jnp.zeros_like(kv)
    keys = jnp.concatenate([jnp.where(low, kv, zero), jnp.where(low, zero, vk)], 0)
    values = jnp.concatenate([jnp.where(low, vk, zero), jnp.where(low, zero, kv)], 0)
    bias = bias_ref[b]
    bias = jnp.concatenate([bias, bias], 1)
    causal = iota((BLOCK, 256), 0) <= lax.rem(iota((BLOCK, 256), 1), BLOCK)
    causal_low = causal.astype(F32).astype(BF16)
    queries, grads, scores = [], [], []
    for quad in range(2):
        c = h * 512 + quad * 256
        qs = jnp.concatenate([q_ref[rows, c : c + 128], q_ref[rows, c + 128 : c + 256]], 0)
        os = jnp.concatenate([o_ref[rows, c : c + 128], o_ref[rows, c + 128 : c + 256]], 0)
        queries.append(qs)
        grads.append(os)
        scores.append((dot(keys, qs, NT), dot(values, os, NT)))
    g_parts, p_parts = ([], []), ([], [])
    for quad in range(2):
        c = h * 512 + quad * 256
        s_all, d_all = scores[quad]
        dq_t = []
        for odd in range(2):
            r = odd * 256
            s = jnp.where(causal, s_all[r : r + 128], s_all[r + 128 : r + 256]) + bias
            w = jnp.exp2((s - jnp.max(s, 0, keepdims=True)) * EXP2_SCALE)
            inv = 1.0 / jnp.sum(w, 0, keepdims=True)
            d = jnp.where(causal, d_all[r : r + 128], d_all[r + 128 : r + 256])
            delta = jnp.sum(w * d, 0, keepdims=True) * inv
            p = w * inv
            g = (p * (d - delta)).astype(BF16)
            p = p.astype(BF16)
            p_own, g_own = p * causal_low, g * causal_low
            p = jnp.concatenate([p_own, p - p_own], 0)
            g = jnp.concatenate([g_own, g - g_own], 0)
            p_parts[odd].append(p)
            g_parts[odd].append(g)
            dq_t.append(dot(kv[:, :64], g, TN))
        dq = jnp.concatenate(dq_t, 0) * SCALE
        dq_ref[rows, c : c + 128] = dq[:, :128].T.astype(BF16)
        dq_ref[rows, c + 128 : c + 256] = dq[:, 128:].T.astype(BF16)
    qs, os = jnp.concatenate(queries, 0), jnp.concatenate(grads, 0)
    k_even = dot(jnp.concatenate(g_parts[0], 1), qs, NN) * SCALE
    k_odd = dot(jnp.concatenate(g_parts[1], 1), qs, NN) * SCALE
    v_even = dot(jnp.concatenate(p_parts[0], 1), os, NN)
    v_odd = dot(jnp.concatenate(p_parts[1], 1), os, NN)
    out = jnp.where(low, k_even, v_odd) + swap_halves(jnp.where(low, v_even, k_odd))
    own_ref[h, rows, :] = out[:BLOCK]
    far_ref[h, rows, :] = out[BLOCK:]


def kernel(
    q_hbm, o_hbm, k_ref, v_ref, parent_ref, start_ref, dq_hbm, dk_ref, dv_ref,
    q_ref, o_ref, dq_ref, win0, win1, win2, win3, own_ref, far_ref, bias_ref, out_buf, in_buf,
    load_sem, store_sem, fwd_send, fwd_recv, back_send, back_recv,
):
    me = lax.axis_index("ctx")
    count = lax.axis_size("ctx")
    core = lax.rem(me, 2)
    wins = (win0, win1, win2, win3)

    def at(step):
        return lax.rem(me + count + step, count)

    barrier = pltpu.get_barrier_semaphore()
    for step in (1, 2, 3, -1, -2, -3):
        pl.semaphore_signal(barrier, inc=1, device_id=(at(step),), device_id_type=MESH)
    loads = [
        pltpu.make_async_copy(q_hbm, q_ref, load_sem.at[0]),
        pltpu.make_async_copy(o_hbm, o_ref, load_sem.at[1]),
    ]
    for copy in loads:
        copy.start()
    OWN, NEAR, MID, FAR = (pl.ds(12, 4), pl.ds(8, 4), pl.ds(4, 4), pl.ds(0, 4))
    for h in range(HEADS):
        lanes = slice(64 * h, 64 * h + 64)
        for b in range(BLOCKS):
            rows = slice(b * BLOCK, (b + 1) * BLOCK)
            wins[h][12 + b] = jnp.concatenate([k_ref[rows, lanes], v_ref[rows, lanes]], 1)
    first = me * BLOCKS
    parents = [parent_ref[first + b] for b in range(BLOCKS)]
    slots = [
        jnp.where(p >= 0, jnp.clip(p - (first - 3 * BLOCKS), 0, 4 * BLOCKS - 1), -1)
        for p in parents
    ]
    for b in range(BLOCKS):
        s = start_ref[first + b]
        s2 = start_ref[jnp.maximum(parents[b], 0)]
        jj, ii = iota((BLOCK, BLOCK), 0), iota((BLOCK, BLOCK), 1)
        upto = jnp.where(s == 0, BLOCK, s)
        from_key = jnp.where(parents[b] >= 0, s2, BLOCK)
        own = jnp.where((jj >= s) == (ii >= s), 0.0, -1e30)
        far = jnp.where((ii < upto) & (jj >= from_key), 0.0, -1e30)
        bias_ref[b] = jnp.where(jj <= ii, own, far)
    pl.semaphore_wait(barrier, 6)

    def fwd(h, src, dst, send, recv, step):
        return pltpu.make_async_remote_copy(
            src_ref=wins[h].at[src], dst_ref=wins[h].at[dst],
            send_sem=fwd_send.at[h, send], recv_sem=fwd_recv.at[h, recv],
            device_id=(at(step),), device_id_type=MESH,
        )

    def send_own(h):
        @pl.when(core == 0)
        def _():
            fwd(h, OWN, FAR, 1, 2, 3).start()
        fwd(h, OWN, NEAR, 0, 0, 1).start()

    def relay(h):
        @pl.when(core == 0)
        def _():
            fwd(h, OWN, NEAR, 0, 0, 1).wait_recv()
            fwd(h, NEAR, FAR, 3, 2, 2).start()
            fwd(h, NEAR, MID, 2, 1, 1).start()

        @pl.when(core == 1)
        def _():
            fwd(h, OWN, FAR, 1, 2, 3).wait_recv()
            fwd(h, FAR, MID, 2, 1, -1).start()

    def ready(h):
        fwd(h, NEAR, MID, 2, 1, 1).wait_recv()

        @pl.when(core == 0)
        def _():
            fwd(h, NEAR, FAR, 3, 2, 2).wait_recv()

        @pl.when(core == 1)
        def _():
            fwd(h, OWN, NEAR, 0, 0, 1).wait_recv()

    def back(h, src, dst, step):
        return pltpu.make_async_remote_copy(
            src_ref=out_buf.at[h, src], dst_ref=in_buf.at[h, dst],
            send_sem=back_send.at[h, src], recv_sem=back_recv.at[h, dst],
            device_id=(at(step),), device_id_type=MESH,
        )

    def window_sum(h, distance, w):
        total = None
        for b in range(BLOCKS):
            if distance == 0 and w >= b:
                continue
            hit = jnp.where(slots[b] == (3 - distance) * BLOCKS + w, 1.0, 0.0)
            term = far_ref[h, b * BLOCK : (b + 1) * BLOCK, :] * hit
            total = term if total is None else total + term
        return total

    def block_rows(w):
        return slice(w * BLOCK, (w + 1) * BLOCK)

    def fill(h, src, distance, arrived):
        for w in range(BLOCKS):
            total = window_sum(h, distance, w)
            for dst in arrived:
                total = total + in_buf[h, dst, block_rows(w), :].astype(F32)
            out_buf[h, src, block_rows(w), :] = total.astype(BF16)

    def give(h):
        @pl.when(core == 0)
        def _():
            fill(h, 0, 3, ())
            back(h, 0, 1, -2).start()
            fill(h, 1, 2, ())
            back(h, 1, 0, 1).start()

        @pl.when(core == 1)
        def _():
            fill(h, 0, 2, ())
            back(h, 0, 0, -1).start()
            fill(h, 1, 1, ())
            back(h, 1, 2, -1).start()

    def merge(h):
        @pl.when(core == 0)
        def _():
            back(h, 0, 0, -1).wait_recv()
            back(h, 0, 1, -2).wait_recv()
            fill(h, 2, 1, (0, 1))
            back(h, 2, 2, -1).start()

        @pl.when(core == 1)
        def _():
            back(h, 1, 0, 1).wait_recv()
            fill(h, 2, 3, (0,))
            back(h, 2, 3, -3).start()

    def take(h):
        for w in range(BLOCKS - 1):
            own_ref[h, block_rows(w), :] += window_sum(h, 0, w)
        back(h, 1, 2, -1).wait_recv()

        @pl.when(core == 0)
        def _():
            back(h, 2, 3, -3).wait_recv()
            own_ref[h] += in_buf[h, 3].astype(F32)
        own_ref[h] += in_buf[h, 2].astype(F32)

    send_own(0)
    send_own(1)
    relay(0)
    send_own(2)
    for copy in loads:
        copy.wait()
    stores = []
    for h in range(HEADS):
        ready(h)

        @pl.loop(0, BLOCKS)
        def _(b, h=h):
            slot = jnp.maximum(parent_ref[first + b] - (first - 3 * BLOCKS), 0)
            own_kv = wins[h][12 + b]
            far_kv = wins[h][slot]
            compute_block(h, b, own_kv, far_kv, q_ref, o_ref, dq_ref, bias_ref, own_ref, far_ref)

            @pl.when(b == 0)
            def _():
                if h + 1 < HEADS:
                    relay(h + 1)
                if h + 3 < HEADS:
                    send_own(h + 3)

            @pl.when(b == 2)
            def _():
                if h > 0:
                    merge(h - 1)

        give(h)
        lanes = pl.ds(512 * h, 512)
        store = pltpu.make_async_copy(dq_ref.at[:, lanes], dq_hbm.at[:, lanes], store_sem.at[h])
        store.start()
        stores.append(store)
    for h in range(HEADS - 1):
        take(h)
    merge(HEADS - 1)
    take(HEADS - 1)
    for h in range(0, HEADS, 2):
        lanes = slice(64 * h, 64 * h + 128)
        a, b = own_ref[h], own_ref[h + 1]
        dk_ref[:, lanes] = jnp.concatenate([a[:, :64], b[:, :64]], 1).astype(BF16)
        dv_ref[:, lanes] = jnp.concatenate([a[:, 64:], b[:, 64:]], 1).astype(BF16)
    for copy in stores:
        copy.wait()
    for h in range(HEADS):
        fwd(h, OWN, NEAR, 0, 0, 1).wait_send()
        fwd(h, NEAR, MID, 2, 1, 1).wait_send()

        @pl.when(core == 0)
        def _():
            fwd(h, OWN, FAR, 1, 2, 3).wait_send()
            fwd(h, NEAR, FAR, 3, 2, 2).wait_send()
        for src in range(3):
            back(h, src, 0, 1).wait_send()


def shards(q, k, v, o, parent_block, seg_start):
    vmem = pl.BlockSpec(memory_space=pltpu.VMEM)
    smem = pl.BlockSpec(memory_space=pltpu.SMEM)
    hbm = pl.BlockSpec(memory_space=pl.ANY)
    width = q.shape[1]
    return pl.pallas_call(
        kernel,
        out_shape=(
            jax.ShapeDtypeStruct(q.shape, BF16),
            jax.ShapeDtypeStruct(k.shape, BF16),
            jax.ShapeDtypeStruct(v.shape, BF16),
        ),
        in_specs=[hbm, hbm, vmem, vmem, smem, smem],
        out_specs=(hbm, vmem, vmem),
        scratch_shapes=[
            pltpu.VMEM((ROWS, width), BF16),
            pltpu.VMEM((ROWS, width), BF16),
            pltpu.VMEM((ROWS, width), BF16),
        ]
        + [pltpu.VMEM((4 * BLOCKS, BLOCK, BLOCK), BF16)] * HEADS
        + [
            pltpu.VMEM((HEADS, ROWS, BLOCK), F32),
            pltpu.VMEM((HEADS, ROWS, BLOCK), F32),
            pltpu.VMEM((BLOCKS, BLOCK, BLOCK), F32),
            pltpu.VMEM((HEADS, 3, ROWS, BLOCK), BF16),
            pltpu.VMEM((HEADS, 4, ROWS, BLOCK), BF16),
            pltpu.SemaphoreType.DMA((2,)),
            pltpu.SemaphoreType.DMA((HEADS,)),
            pltpu.SemaphoreType.DMA((HEADS, 4)),
            pltpu.SemaphoreType.DMA((HEADS, 3)),
            pltpu.SemaphoreType.DMA((HEADS, 3)),
            pltpu.SemaphoreType.DMA((HEADS, 4)),
        ],
        compiler_params=pltpu.CompilerParams(
            collective_id=0, has_side_effects=True, vmem_limit_bytes=48 * 2**20
        ),
    )(q, o, k, v, parent_block, seg_start)


def solution(mesh):
    rows = P("ctx", None)
    return jax.shard_map(
        shards,
        mesh=mesh,
        in_specs=(rows, rows, rows, rows, P(), P()),
        out_specs=(rows, rows, rows),
        check_vma=False,
    )
```

```python
import jax
import jax.numpy as jnp
from jax import lax
from jax.experimental import pallas as pl
from jax.experimental.pallas import tpu as pltpu
from jax.sharding import PartitionSpec as P

HEADS = 4
BLOCK = 128
BLOCKS = 4
ROWS = BLOCK * BLOCKS
F32, BF16 = jnp.float32, jnp.bfloat16
SCALE = 0.125
EXP2_SCALE = SCALE * 1.4426950408889634
NT = (((1,), (1,)), ((), ()))
NN = (((1,), (0,)), ((), ()))
TN = (((0,), (0,)), ((), ()))
MESH = pl.DeviceIdType.MESH
OWN, NEAR, MID, FAR = 12, 8, 4, 0
FWD_PARTS = (4, 1, 1, 1)
BACK_PARTS = (1, 1, 1, 4)


def dot(a, b, dims):
    return lax.dot_general(a, b, dims, preferred_element_type=F32)


def iota(shape, dim):
    return lax.broadcasted_iota(jnp.int32, shape, dim)


def swap_halves(x):
    return jnp.concatenate([x[:, 64:], x[:, :64]], 1)


def compute_block(h, b, own_kv, far_kv, q_ref, o_ref, dq_ref, bias_ref, own_ref, far_ref):
    rows = pl.ds(pl.multiple_of(b * BLOCK, BLOCK), BLOCK)
    kv = jnp.concatenate([own_kv, far_kv], 0)
    vk = swap_halves(kv)
    low = iota((256, 128), 1) < 64
    zero = jnp.zeros_like(kv)
    keys = jnp.concatenate([jnp.where(low, kv, zero), jnp.where(low, zero, vk)], 0)
    values = jnp.concatenate([jnp.where(low, vk, zero), jnp.where(low, zero, kv)], 0)
    bias = bias_ref[b]
    bias = jnp.concatenate([bias, bias], 1)
    causal = iota((BLOCK, 256), 0) <= lax.rem(iota((BLOCK, 256), 1), BLOCK)
    causal_low = causal.astype(F32).astype(BF16)
    queries, grads, scores = [], [], []
    for quad in range(2):
        c = h * 512 + quad * 256
        qs = jnp.concatenate([q_ref[rows, c : c + 128], q_ref[rows, c + 128 : c + 256]], 0)
        os = jnp.concatenate([o_ref[rows, c : c + 128], o_ref[rows, c + 128 : c + 256]], 0)
        queries.append(qs)
        grads.append(os)
        scores.append((dot(keys, qs, NT), dot(values, os, NT)))
    g_parts, p_parts = ([], []), ([], [])
    for quad in range(2):
        c = h * 512 + quad * 256
        s_all, d_all = scores[quad]
        dq_t = []
        for odd in range(2):
            r = odd * 256
            s = jnp.where(causal, s_all[r : r + 128], s_all[r + 128 : r + 256]) + bias
            w = jnp.exp2((s - jnp.max(s, 0, keepdims=True)) * EXP2_SCALE)
            inv = 1.0 / jnp.sum(w, 0, keepdims=True)
            d = jnp.where(causal, d_all[r : r + 128], d_all[r + 128 : r + 256])
            delta = jnp.sum(w * d, 0, keepdims=True) * inv
            p = w * inv
            g = (p * (d - delta)).astype(BF16)
            p = p.astype(BF16)
            p_own, g_own = p * causal_low, g * causal_low
            p = jnp.concatenate([p_own, p - p_own], 0)
            g = jnp.concatenate([g_own, g - g_own], 0)
            p_parts[odd].append(p)
            g_parts[odd].append(g)
            dq_t.append(dot(kv[:, :64], g, TN))
        dq = jnp.concatenate(dq_t, 0) * SCALE
        dq_ref[rows, c : c + 128] = dq[:, :128].T.astype(BF16)
        dq_ref[rows, c + 128 : c + 256] = dq[:, 128:].T.astype(BF16)
    qs, os = jnp.concatenate(queries, 0), jnp.concatenate(grads, 0)
    k_even = dot(jnp.concatenate(g_parts[0], 1), qs, NN) * SCALE
    k_odd = dot(jnp.concatenate(g_parts[1], 1), qs, NN) * SCALE
    v_even = dot(jnp.concatenate(p_parts[0], 1), os, NN)
    v_odd = dot(jnp.concatenate(p_parts[1], 1), os, NN)
    out = jnp.where(low, k_even, v_odd) + swap_halves(jnp.where(low, v_even, k_odd))
    own_ref[h, rows, :] = out[:BLOCK]
    far_ref[h, rows, :] = out[BLOCK:]


def kernel(
    q_hbm, o_hbm, k_hbm, v_hbm, parent_hbm, start_hbm, dq_ref, dk_ref, dv_ref,
    k_ref, v_ref, parent_ref, start_ref, q_ref, o_ref, win0, win1, win2, win3, own_ref, far_ref, bias_ref, out_buf, in_buf,
    load_sem, fwd_send, fwd_recv, back_send, back_recv,
):
    me = lax.axis_index("ctx")
    count = lax.axis_size("ctx")
    core = lax.rem(me, 2)
    wins = (win0, win1, win2, win3)

    def at(step):
        return lax.rem(me + count + step, count)

    barrier = pltpu.get_barrier_semaphore()
    for step in (1, 2, 3, -1, -2, -3):
        pl.semaphore_signal(barrier, inc=1, device_id=(at(step),), device_id_type=MESH)
    loads = [
        pltpu.make_async_copy(src, dst, load_sem.at[n])
        for n, (src, dst) in enumerate(
            (
                (k_hbm, k_ref), (v_hbm, v_ref), (parent_hbm, parent_ref),
                (start_hbm, start_ref), (q_hbm, q_ref), (o_hbm, o_ref),
            )
        )
    ]
    for copy in loads:
        copy.start()
    for copy in loads[:2]:
        copy.wait()

    def pack(h):
        lanes = slice(64 * h, 64 * h + 64)
        for b in range(BLOCKS):
            rows = slice(b * BLOCK, (b + 1) * BLOCK)
            wins[h][12 + b] = jnp.concatenate([k_ref[rows, lanes], v_ref[rows, lanes]], 1)
    pack(0)
    pl.semaphore_wait(barrier, 6)

    def fwd(h, part, src, dst, send, recv, step):
        size = BLOCKS // FWD_PARTS[h]
        return pltpu.make_async_remote_copy(
            src_ref=wins[h].at[pl.ds(src + part * size, size)],
            dst_ref=wins[h].at[pl.ds(dst + part * size, size)],
            send_sem=fwd_send.at[h, send, part], recv_sem=fwd_recv.at[h, recv, part],
            device_id=(at(step),), device_id_type=MESH,
        )

    def own_far(h, part):
        return fwd(h, part, OWN, FAR, 1, 2, 3)

    def own_near(h, part):
        return fwd(h, part, OWN, NEAR, 0, 0, 1)

    def near_far(h, part):
        return fwd(h, part, NEAR, FAR, 3, 2, 2)

    def near_mid(h, part):
        return fwd(h, part, NEAR, MID, 2, 1, 1)

    def far_mid(h, part):
        return fwd(h, part, FAR, MID, 2, 1, -1)

    def send_own(h, far=True, near=True):
        if far:
            @pl.when(core == 0)
            def _():
                for part in range(FWD_PARTS[h]):
                    own_far(h, part).start()
        if near:
            for part in range(FWD_PARTS[h]):
                own_near(h, part).start()

    def relay(h):
        @pl.when(core == 0)
        def _():
            for part in range(FWD_PARTS[h]):
                own_near(h, part).wait_recv()
                near_far(h, part).start()
                near_mid(h, part).start()

        @pl.when(core == 1)
        def _():
            for part in range(FWD_PARTS[h]):
                own_far(h, part).wait_recv()
                far_mid(h, part).start()

    def ready(h):
        for part in range(FWD_PARTS[h]):
            near_mid(h, part).wait_recv()

            @pl.when(core == 0)
            def _():
                near_far(h, part).wait_recv()

            @pl.when(core == 1)
            def _():
                own_near(h, part).wait_recv()

    def back(h, part, src, dst, step):
        size = ROWS // BACK_PARTS[h]
        rows = pl.ds(part * size, size)
        return pltpu.make_async_remote_copy(
            src_ref=out_buf.at[h, src, rows], dst_ref=in_buf.at[h, dst, rows],
            send_sem=back_send.at[h, src, part], recv_sem=back_recv.at[h, dst, part],
            device_id=(at(step),), device_id_type=MESH,
        )

    def window_sum(h, distance, w):
        total = None
        for b in range(BLOCKS):
            if distance == 0 and w >= b:
                continue
            hit = jnp.where(slots[b] == (3 - distance) * BLOCKS + w, 1.0, 0.0)
            term = far_ref[h, b * BLOCK : (b + 1) * BLOCK, :] * hit
            total = term if total is None else total + term
        return total

    def block_rows(w):
        return slice(w * BLOCK, (w + 1) * BLOCK)

    def send(h, src, dst, step, distance, arrived):
        size = BLOCKS // BACK_PARTS[h]
        for part in range(BACK_PARTS[h]):
            for other in arrived:
                back(h, part, 0, other, 1).wait_recv()
            for w in range(part * size, (part + 1) * size):
                total = window_sum(h, distance, w)
                for other in arrived:
                    total = total + in_buf[h, other, block_rows(w), :].astype(F32)
                out_buf[h, src, block_rows(w), :] = total.astype(BF16)
            back(h, part, src, dst, step).start()

    def give(h):
        @pl.when(core == 0)
        def _():
            send(h, 0, 1, -2, 3, ())
            send(h, 1, 0, 1, 2, ())

        @pl.when(core == 1)
        def _():
            send(h, 0, 0, -1, 2, ())
            send(h, 1, 2, -1, 1, ())

    def merge_even(h):
        @pl.when(core == 0)
        def _():
            send(h, 2, 2, -1, 1, (0, 1))

    def merge_odd(h):
        @pl.when(core == 1)
        def _():
            send(h, 2, 3, -3, 3, (0,))

    def take(h):
        for w in range(BLOCKS - 1):
            own_ref[h, block_rows(w), :] += window_sum(h, 0, w)

        @pl.when(core == 0)
        def _():
            for part in range(BACK_PARTS[h]):
                back(h, part, 2, 3, -3).wait_recv()
            own_ref[h] += in_buf[h, 3].astype(F32)
        for part in range(BACK_PARTS[h]):
            back(h, part, 1, 2, -1).wait_recv()
        own_ref[h] += in_buf[h, 2].astype(F32)

    send_own(0)
    pack(1)
    send_own(1)
    pack(2)
    pack(3)
    for copy in loads[2:]:
        copy.wait()
    first = me * BLOCKS
    parents = [parent_ref[first + b] for b in range(BLOCKS)]
    slots = [
        jnp.where(p >= 0, jnp.clip(p - (first - 3 * BLOCKS), 0, 4 * BLOCKS - 1), -1)
        for p in parents
    ]
    for b in range(BLOCKS):
        s = start_ref[first + b]
        s2 = start_ref[jnp.maximum(parents[b], 0)]
        jj, ii = iota((BLOCK, BLOCK), 0), iota((BLOCK, BLOCK), 1)
        upto = jnp.where(s == 0, BLOCK, s)
        from_key = jnp.where(parents[b] >= 0, s2, BLOCK)
        own = jnp.where((jj >= s) == (ii >= s), 0.0, -1e30)
        far = jnp.where((ii < upto) & (jj >= from_key), 0.0, -1e30)
        bias_ref[b] = jnp.where(jj <= ii, own, far)
    relay(0)
    send_own(2, near=False)
    relay(1)
    send_own(2, far=False)
    send_own(3)
    for h in range(HEADS):
        ready(h)
        if h == 2:
            merge_even(0)

        @pl.loop(0, BLOCKS // 2)
        def _(pair, h=h):
            for b in (2 * pair, 2 * pair + 1):
                slot = jnp.maximum(parent_ref[first + b] - (first - 3 * BLOCKS), 0)
                compute_block(
                    h, b, wins[h][12 + b], wins[h][slot], q_ref, o_ref, dq_ref, bias_ref, own_ref, far_ref
                )

            @pl.when(pair == 0)
            def _():
                if h > 0:
                    merge_odd(h - 1)

        if h < 2:
            relay(h + 2)
        give(h)
        if h == 2:
            merge_even(1)
    merge_odd(3)
    merge_even(2)
    take(0)
    take(1)
    merge_even(3)
    take(2)
    take(3)
    for h in range(0, HEADS, 2):
        lanes = slice(64 * h, 64 * h + 128)
        a, b = own_ref[h], own_ref[h + 1]
        dk_ref[:, lanes] = jnp.concatenate([a[:, :64], b[:, :64]], 1).astype(BF16)
        dv_ref[:, lanes] = jnp.concatenate([a[:, 64:], b[:, 64:]], 1).astype(BF16)
    for h in range(HEADS):
        for part in range(FWD_PARTS[h]):
            own_near(h, part).wait_send()
            near_mid(h, part).wait_send()

            @pl.when(core == 0)
            def _():
                own_far(h, part).wait_send()
                near_far(h, part).wait_send()
        for part in range(BACK_PARTS[h]):
            for src in range(3):
                back(h, part, src, 0, 1).wait_send()


def shards(q, k, v, o, parent_block, seg_start):
    hbm = pl.BlockSpec(memory_space=pltpu.HBM)
    vmem = pl.BlockSpec(memory_space=pltpu.VMEM)
    width = q.shape[1]
    return pl.pallas_call(
        kernel,
        out_shape=(
            jax.ShapeDtypeStruct(q.shape, BF16),
            jax.ShapeDtypeStruct(k.shape, BF16),
            jax.ShapeDtypeStruct(v.shape, BF16),
        ),
        in_specs=[hbm] * 6,
        out_specs=(vmem,) * 3,
        scratch_shapes=[
            pltpu.VMEM(k.shape, BF16),
            pltpu.VMEM(v.shape, BF16),
            pltpu.SMEM(parent_block.shape, jnp.int32),
            pltpu.SMEM(seg_start.shape, jnp.int32),
            pltpu.VMEM((ROWS, width), BF16),
            pltpu.VMEM((ROWS, width), BF16),
        ]
        + [pltpu.VMEM((4 * BLOCKS, BLOCK, BLOCK), BF16)] * HEADS
        + [
            pltpu.VMEM((HEADS, ROWS, BLOCK), F32),
            pltpu.VMEM((HEADS, ROWS, BLOCK), F32),
            pltpu.VMEM((BLOCKS, BLOCK, BLOCK), F32),
            pltpu.VMEM((HEADS, 3, ROWS, BLOCK), BF16),
            pltpu.VMEM((HEADS, 4, ROWS, BLOCK), BF16),
            pltpu.SemaphoreType.DMA((6,)),
            pltpu.SemaphoreType.DMA((HEADS, 4, 4)),
            pltpu.SemaphoreType.DMA((HEADS, 3, 4)),
            pltpu.SemaphoreType.DMA((HEADS, 3, 4)),
            pltpu.SemaphoreType.DMA((HEADS, 4, 4)),
        ],
        compiler_params=pltpu.CompilerParams(
            collective_id=0, has_side_effects=True, vmem_limit_bytes=48 * 2**20
        ),
    )(*(pltpu.with_memory_space_constraint(x, pltpu.HBM) for x in (q, o, k, v, parent_block, seg_start)))


def solution(mesh):
    rows = P("ctx", None)
    return jax.shard_map(
        shards,
        mesh=mesh,
        in_specs=(rows, rows, rows, rows, P(), P()),
        out_specs=(rows, rows, rows),
        check_vma=False,
    )
```

```python
import jax
import jax.numpy as jnp
from jax import lax
from jax.experimental import pallas as pl
from jax.experimental.pallas import tpu as pltpu
from jax.sharding import PartitionSpec as P

HEADS = 4
BLOCK = 128
BLOCKS = 4
ROWS = BLOCK * BLOCKS
F32, BF16 = jnp.float32, jnp.bfloat16
SCALE = 0.125
EXP2_SCALE = SCALE * 1.4426950408889634
NT = (((1,), (1,)), ((), ()))
NN = (((1,), (0,)), ((), ()))
TN = (((0,), (0,)), ((), ()))
MESH = pl.DeviceIdType.MESH
OWN, NEAR, MID, FAR = 12, 8, 4, 0
FWD_PARTS = (4, 1, 1, 1)
BACK_PARTS = (1, 1, 1, 4)


def dot(a, b, dims):
    return lax.dot_general(a, b, dims, preferred_element_type=F32)


def iota(shape, dim):
    return lax.broadcasted_iota(jnp.int32, shape, dim)


def swap_halves(x):
    return jnp.concatenate([x[:, 64:], x[:, :64]], 1)


def compute_block(h, b, own_kv, far_kv, q_ref, o_ref, dq_ref, bias_ref, own_ref, far_ref):
    rows = slice(b * BLOCK, (b + 1) * BLOCK)
    kv = jnp.concatenate([own_kv, far_kv], 0)
    vk = swap_halves(kv)
    low = iota((256, 128), 1) < 64
    zero = jnp.zeros_like(kv)
    keys = jnp.concatenate([jnp.where(low, kv, zero), jnp.where(low, zero, vk)], 0)
    values = jnp.concatenate([jnp.where(low, vk, zero), jnp.where(low, zero, kv)], 0)
    bias = bias_ref[b]
    bias = jnp.concatenate([bias, bias], 1)
    causal = iota((BLOCK, 256), 0) <= lax.rem(iota((BLOCK, 256), 1), BLOCK)
    causal_low = causal.astype(F32).astype(BF16)
    queries, grads, scores = [], [], []
    for quad in range(2):
        c = h * 512 + quad * 256
        qs = jnp.concatenate([q_ref[rows, c : c + 128], q_ref[rows, c + 128 : c + 256]], 0)
        os = jnp.concatenate([o_ref[rows, c : c + 128], o_ref[rows, c + 128 : c + 256]], 0)
        queries.append(qs)
        grads.append(os)
        scores.append((dot(keys, qs, NT), dot(values, os, NT)))
    g_parts, p_parts = ([], []), ([], [])
    for quad in range(2):
        c = h * 512 + quad * 256
        s_all, d_all = scores[quad]
        dq_t = []
        for odd in range(2):
            r = odd * 256
            s = jnp.where(causal, s_all[r : r + 128], s_all[r + 128 : r + 256]) + bias
            w = jnp.exp2((s - jnp.max(s, 0, keepdims=True)) * EXP2_SCALE)
            inv = 1.0 / jnp.sum(w, 0, keepdims=True)
            d = jnp.where(causal, d_all[r : r + 128], d_all[r + 128 : r + 256])
            delta = jnp.sum(w * d, 0, keepdims=True) * inv
            p = w * inv
            g = (p * (d - delta)).astype(BF16)
            p = p.astype(BF16)
            p_own, g_own = p * causal_low, g * causal_low
            p = jnp.concatenate([p_own, p - p_own], 0)
            g = jnp.concatenate([g_own, g - g_own], 0)
            p_parts[odd].append(p)
            g_parts[odd].append(g)
            dq_t.append(dot(kv[:, :64], g, TN))
        dq = jnp.concatenate(dq_t, 0) * SCALE
        dq_ref[rows, c : c + 128] = dq[:, :128].T.astype(BF16)
        dq_ref[rows, c + 128 : c + 256] = dq[:, 128:].T.astype(BF16)
    qs, os = jnp.concatenate(queries, 0), jnp.concatenate(grads, 0)
    k_even = dot(jnp.concatenate(g_parts[0], 1), qs, NN) * SCALE
    k_odd = dot(jnp.concatenate(g_parts[1], 1), qs, NN) * SCALE
    v_even = dot(jnp.concatenate(p_parts[0], 1), os, NN)
    v_odd = dot(jnp.concatenate(p_parts[1], 1), os, NN)
    out = jnp.where(low, k_even, v_odd) + swap_halves(jnp.where(low, v_even, k_odd))
    own_ref[h, rows, :] = out[:BLOCK]
    far_ref[h, rows, :] = out[BLOCK:]


def kernel(
    q_hbm, o_hbm, k_hbm, v_hbm, parent_hbm, start_hbm, dq_ref, dk_ref, dv_ref,
    k_ref, v_ref, parent_ref, start_ref, q_ref, o_ref, win0, win1, win2, win3, own_ref, far_ref, bias_ref, out_buf, in_buf,
    load_sem, fwd_send, fwd_recv, back_send, back_recv,
):
    me = lax.axis_index("ctx")
    count = lax.axis_size("ctx")
    core = lax.rem(me, 2)
    wins = (win0, win1, win2, win3)

    chip, last = me // 2, count // 2 - 1
    even, odd = core == 0, core == 1
    prev, prev2, later = chip > 0, chip > 1, chip < last

    def at(step):
        return lax.rem(me + count + step, count)

    barrier = pltpu.get_barrier_semaphore()
    for step in (1, 2, 3, -1, -2, -3):
        @pl.when(me + step < count if step > 0 else me + step >= 0)
        def _():
            pl.semaphore_signal(barrier, inc=1, device_id=(at(step),), device_id_type=MESH)
    loads = [
        pltpu.make_async_copy(src, dst, load_sem.at[n])
        for n, (src, dst) in enumerate(
            (
                (k_hbm, k_ref), (v_hbm, v_ref), (parent_hbm, parent_ref),
                (start_hbm, start_ref), (q_hbm, q_ref), (o_hbm, o_ref),
            )
        )
    ]
    for copy in loads:
        copy.start()
    for copy in loads[:2]:
        copy.wait()

    def pack(h):
        lanes = slice(64 * h, 64 * h + 64)
        for b in range(BLOCKS):
            rows = slice(b * BLOCK, (b + 1) * BLOCK)
            wins[h][12 + b] = jnp.concatenate([k_ref[rows, lanes], v_ref[rows, lanes]], 1)
    pack(0)
    pl.semaphore_wait(barrier, jnp.minimum(me, 3) + jnp.minimum(count - 1 - me, 3))

    def fwd(h, part, src, dst, send, recv, step):
        size = BLOCKS // FWD_PARTS[h]
        return pltpu.make_async_remote_copy(
            src_ref=wins[h].at[pl.ds(src + part * size, size)],
            dst_ref=wins[h].at[pl.ds(dst + part * size, size)],
            send_sem=fwd_send.at[h, send, part], recv_sem=fwd_recv.at[h, recv, part],
            device_id=(at(step),), device_id_type=MESH,
        )

    def own_far(h, part):
        return fwd(h, part, OWN, FAR, 1, 2, 3)

    def own_near(h, part):
        return fwd(h, part, OWN, NEAR, 0, 0, 1)

    def near_far(h, part):
        return fwd(h, part, NEAR, FAR, 3, 2, 2)

    def near_mid(h, part):
        return fwd(h, part, NEAR, MID, 2, 1, 1)

    def far_mid(h, part):
        return fwd(h, part, FAR, MID, 2, 1, -1)

    def send_own(h, far=True, near=True):
        if far:
            @pl.when(even & later)
            def _():
                for part in range(FWD_PARTS[h]):
                    own_far(h, part).start()
        if near:
            @pl.when(even | later)
            def _():
                for part in range(FWD_PARTS[h]):
                    own_near(h, part).start()

    def relay(h):
        @pl.when(even & prev)
        def _():
            for part in range(FWD_PARTS[h]):
                own_near(h, part).wait_recv()

                @pl.when(later)
                def _():
                    near_far(h, part).start()
                near_mid(h, part).start()

        @pl.when(odd & prev)
        def _():
            for part in range(FWD_PARTS[h]):
                own_far(h, part).wait_recv()
                far_mid(h, part).start()

    def ready(h):
        for part in range(FWD_PARTS[h]):
            @pl.when(odd)
            def _():
                own_near(h, part).wait_recv()

            @pl.when(prev)
            def _():
                near_mid(h, part).wait_recv()

            @pl.when(even & prev2)
            def _():
                near_far(h, part).wait_recv()

    def back(h, part, src, dst, step):
        size = ROWS // BACK_PARTS[h]
        rows = pl.ds(part * size, size)
        return pltpu.make_async_remote_copy(
            src_ref=out_buf.at[h, src, rows], dst_ref=in_buf.at[h, dst, rows],
            send_sem=back_send.at[h, src, part], recv_sem=back_recv.at[h, dst, part],
            device_id=(at(step),), device_id_type=MESH,
        )

    def window_sum(h, distance, w):
        total = None
        for b in range(BLOCKS):
            if distance == 0 and w >= b:
                continue
            hit = jnp.where(slots[b] == (3 - distance) * BLOCKS + w, 1.0, 0.0)
            term = far_ref[h, b * BLOCK : (b + 1) * BLOCK, :] * hit
            total = term if total is None else total + term
        return total

    def block_rows(w):
        return slice(w * BLOCK, (w + 1) * BLOCK)

    def send(h, src, dst, step, distance, arrived):
        size = BLOCKS // BACK_PARTS[h]
        for part in range(BACK_PARTS[h]):
            for other in arrived:
                back(h, part, 0, other, 1).wait_recv()
            for w in range(part * size, (part + 1) * size):
                total = window_sum(h, distance, w)
                for other in arrived:
                    total = total + in_buf[h, other, block_rows(w), :].astype(F32)
                out_buf[h, src, block_rows(w), :] = total.astype(BF16)
            back(h, part, src, dst, step).start()

    def give(h):
        @pl.when(even & prev2)
        def _():
            send(h, 0, 1, -2, 3, ())

        @pl.when(even & prev)
        def _():
            send(h, 1, 0, 1, 2, ())

        @pl.when(odd & prev)
        def _():
            send(h, 0, 0, -1, 2, ())

        @pl.when(odd)
        def _():
            send(h, 1, 2, -1, 1, ())

    def merge_even(h):
        @pl.when(even & prev & later)
        def _():
            send(h, 2, 2, -1, 1, (0, 1))

        @pl.when(even & prev & (chip == last))
        def _():
            send(h, 2, 2, -1, 1, (0,))

    def merge_odd(h):
        @pl.when(odd & prev)
        def _():
            send(h, 2, 3, -3, 3, (0,))

    def take(h):
        for w in range(BLOCKS - 1):
            own_ref[h, block_rows(w), :] += window_sum(h, 0, w)

        @pl.when(even & later)
        def _():
            for part in range(BACK_PARTS[h]):
                back(h, part, 2, 3, -3).wait_recv()
            own_ref[h] += in_buf[h, 3].astype(F32)

        @pl.when(even | later)
        def _():
            for part in range(BACK_PARTS[h]):
                back(h, part, 1, 2, -1).wait_recv()
            own_ref[h] += in_buf[h, 2].astype(F32)

    send_own(0)
    pack(1)
    send_own(1)
    pack(2)
    pack(3)
    for copy in loads[2:]:
        copy.wait()
    first = me * BLOCKS
    oldest = jnp.maximum(3 * BLOCKS - first, 0)
    parents = [parent_ref[first + b] for b in range(BLOCKS)]
    slots = [
        jnp.where(p >= 0, jnp.clip(p - (first - 3 * BLOCKS), 0, 4 * BLOCKS - 1), -1)
        for p in parents
    ]
    for b in range(BLOCKS):
        s = start_ref[first + b]
        s2 = start_ref[jnp.maximum(parents[b], 0)]
        jj, ii = iota((BLOCK, BLOCK), 0), iota((BLOCK, BLOCK), 1)
        upto = jnp.where(s == 0, BLOCK, s)
        from_key = jnp.where(parents[b] >= 0, s2, BLOCK)
        own = jnp.where((jj >= s) == (ii >= s), 0.0, -1e30)
        far = jnp.where((ii < upto) & (jj >= from_key), 0.0, -1e30)
        bias_ref[b] = jnp.where(jj <= ii, own, far)
    relay(0)
    send_own(2, near=False)
    relay(1)
    send_own(2, far=False)
    send_own(3)
    for h in range(HEADS):
        ready(h)
        if h == 2:
            merge_even(0)
        if h == 3:
            merge_odd(2)
        for b in range(BLOCKS):
            slot = jnp.maximum(parent_ref[first + b] - (first - 3 * BLOCKS), oldest)
            compute_block(
                h, b, wins[h][12 + b], wins[h][slot], q_ref, o_ref, dq_ref, bias_ref, own_ref, far_ref
            )
        if h in (1, 2):
            merge_odd(h - 1)
        if h < 2:
            relay(h + 2)
        give(h)
        if h == 2:
            merge_even(1)
    merge_odd(3)
    merge_even(2)
    take(0)
    take(1)
    merge_even(3)
    take(2)
    take(3)
    for h in range(0, HEADS, 2):
        lanes = slice(64 * h, 64 * h + 128)
        a, b = own_ref[h], own_ref[h + 1]
        dk_ref[:, lanes] = jnp.concatenate([a[:, :64], b[:, :64]], 1).astype(BF16)
        dv_ref[:, lanes] = jnp.concatenate([a[:, 64:], b[:, 64:]], 1).astype(BF16)
    for h in range(HEADS):
        for part in range(FWD_PARTS[h]):
            @pl.when(even | later)
            def _():
                own_near(h, part).wait_send()

            @pl.when(even & later)
            def _():
                own_far(h, part).wait_send()

            @pl.when(prev)
            def _():
                near_mid(h, part).wait_send()

            @pl.when(even & prev & later)
            def _():
                near_far(h, part).wait_send()
        for part in range(BACK_PARTS[h]):
            @pl.when(odd | prev)
            def _():
                back(h, part, 1, 0, 1).wait_send()

            @pl.when((odd & prev) | prev2)
            def _():
                back(h, part, 0, 0, 1).wait_send()

            @pl.when(prev)
            def _():
                back(h, part, 2, 0, 1).wait_send()


def shards(q, k, v, o, parent_block, seg_start):
    hbm = pl.BlockSpec(memory_space=pltpu.HBM)
    vmem = pl.BlockSpec(memory_space=pltpu.VMEM)
    width = q.shape[1]
    return pl.pallas_call(
        kernel,
        out_shape=(
            jax.ShapeDtypeStruct(q.shape, BF16),
            jax.ShapeDtypeStruct(k.shape, BF16),
            jax.ShapeDtypeStruct(v.shape, BF16),
        ),
        in_specs=[hbm] * 6,
        out_specs=(vmem,) * 3,
        scratch_shapes=[
            pltpu.VMEM(k.shape, BF16),
            pltpu.VMEM(v.shape, BF16),
            pltpu.SMEM(parent_block.shape, jnp.int32),
            pltpu.SMEM(seg_start.shape, jnp.int32),
            pltpu.VMEM((ROWS, width), BF16),
            pltpu.VMEM((ROWS, width), BF16),
        ]
        + [pltpu.VMEM((4 * BLOCKS, BLOCK, BLOCK), BF16)] * HEADS
        + [
            pltpu.VMEM((HEADS, ROWS, BLOCK), F32),
            pltpu.VMEM((HEADS, ROWS, BLOCK), F32),
            pltpu.VMEM((BLOCKS, BLOCK, BLOCK), F32),
            pltpu.VMEM((HEADS, 3, ROWS, BLOCK), BF16),
            pltpu.VMEM((HEADS, 4, ROWS, BLOCK), BF16),
            pltpu.SemaphoreType.DMA((6,)),
            pltpu.SemaphoreType.DMA((HEADS, 4, 4)),
            pltpu.SemaphoreType.DMA((HEADS, 3, 4)),
            pltpu.SemaphoreType.DMA((HEADS, 3, 4)),
            pltpu.SemaphoreType.DMA((HEADS, 4, 4)),
        ],
        compiler_params=pltpu.CompilerParams(
            collective_id=0, has_side_effects=True, vmem_limit_bytes=48 * 2**20
        ),
    )(*(pltpu.with_memory_space_constraint(x, pltpu.HBM) for x in (q, o, k, v, parent_block, seg_start)))


def solution(mesh):
    rows = P("ctx", None)
    return jax.shard_map(
        shards,
        mesh=mesh,
        in_specs=(rows, rows, rows, rows, P(), P()),
        out_specs=(rows, rows, rows),
        check_vma=False,
    )
```

```python
import jax
import jax.numpy as jnp
from jax import lax
from jax.experimental import pallas as pl
from jax.experimental.pallas import tpu as pltpu
from jax.sharding import PartitionSpec as P

HEADS = 4
BLOCK = 128
BLOCKS = 4
ROWS = BLOCK * BLOCKS
F32, BF16 = jnp.float32, jnp.bfloat16
SCALE = 0.125
EXP2_SCALE = SCALE * 1.4426950408889634
NT = (((1,), (1,)), ((), ()))
NN = (((1,), (0,)), ((), ()))
TN = (((0,), (0,)), ((), ()))
MESH = pl.DeviceIdType.MESH
OWN, NEAR, MID, FAR = 12, 8, 4, 0
FWD_PARTS = (4, 1, 1, 1)
BACK_PARTS = (1, 1, 1, 4)


def dot(a, b, dims):
    return lax.dot_general(a, b, dims, preferred_element_type=F32)


def iota(shape, dim):
    return lax.broadcasted_iota(jnp.int32, shape, dim)


def swap_halves(x):
    return jnp.concatenate([x[:, 64:], x[:, :64]], 1)


def compute_block(h, b, own_kv, far_kv, q_ref, o_ref, dq_ref, bias_ref, own_ref, far_ref):
    rows = slice(b * BLOCK, (b + 1) * BLOCK)
    kv = jnp.concatenate([own_kv, far_kv], 0)
    vk = swap_halves(kv)
    low = iota((256, 128), 1) < 64
    zero = jnp.zeros_like(kv)
    keys = jnp.concatenate([jnp.where(low, kv, zero), jnp.where(low, zero, vk)], 0)
    values = jnp.concatenate([jnp.where(low, vk, zero), jnp.where(low, zero, kv)], 0)
    bias = bias_ref[b]
    bias = jnp.concatenate([bias, bias], 1)
    causal = iota((BLOCK, 256), 0) <= lax.rem(iota((BLOCK, 256), 1), BLOCK)
    causal_low = causal.astype(F32).astype(BF16)
    queries, grads, scores = [], [], []
    for quad in range(2):
        c = h * 512 + quad * 256
        qs = jnp.concatenate([q_ref[rows, c : c + 128], q_ref[rows, c + 128 : c + 256]], 0)
        os = jnp.concatenate([o_ref[rows, c : c + 128], o_ref[rows, c + 128 : c + 256]], 0)
        queries.append(qs)
        grads.append(os)
        scores.append((dot(keys, qs, NT), dot(values, os, NT)))
    g_parts, p_parts = ([], []), ([], [])
    for quad in range(2):
        c = h * 512 + quad * 256
        s_all, d_all = scores[quad]
        dq_t = []
        for odd in range(2):
            r = odd * 256
            s = jnp.where(causal, s_all[r : r + 128], s_all[r + 128 : r + 256]) + bias
            w = jnp.exp2((s - jnp.max(s, 0, keepdims=True)) * EXP2_SCALE)
            inv = 1.0 / jnp.sum(w, 0, keepdims=True)
            d = jnp.where(causal, d_all[r : r + 128], d_all[r + 128 : r + 256])
            delta = jnp.sum(w * d, 0, keepdims=True) * inv
            p = w * inv
            g = (p * (d - delta)).astype(BF16)
            p = p.astype(BF16)
            p_own, g_own = p * causal_low, g * causal_low
            p = jnp.concatenate([p_own, p - p_own], 0)
            g = jnp.concatenate([g_own, g - g_own], 0)
            p_parts[odd].append(p)
            g_parts[odd].append(g)
            dq_t.append(dot(kv[:, :64], g, TN))
        dq = jnp.concatenate(dq_t, 0) * SCALE
        dq_ref[rows, c : c + 128] = dq[:, :128].T.astype(BF16)
        dq_ref[rows, c + 128 : c + 256] = dq[:, 128:].T.astype(BF16)
    qs, os = jnp.concatenate(queries, 0), jnp.concatenate(grads, 0)
    k_even = dot(jnp.concatenate(g_parts[0], 1), qs, NN) * SCALE
    k_odd = dot(jnp.concatenate(g_parts[1], 1), qs, NN) * SCALE
    v_even = dot(jnp.concatenate(p_parts[0], 1), os, NN)
    v_odd = dot(jnp.concatenate(p_parts[1], 1), os, NN)
    out = jnp.where(low, k_even, v_odd) + swap_halves(jnp.where(low, v_even, k_odd))
    own_ref[h, rows, :] = out[:BLOCK]
    far_ref[h, rows, :] = out[BLOCK:]


def kernel(
    q_hbm, o_hbm, k_hbm, v_hbm, parent_hbm, start_hbm, dq_ref, dk_ref, dv_ref,
    k_ref, v_ref, parent_ref, start_ref, q_ref, o_ref, win0, win1, win2, win3, own_ref, far_ref, bias_ref, out_buf, in_buf,
    load_sem, fwd_send, fwd_recv, back_send, back_recv,
):
    me = lax.axis_index("ctx")
    count = lax.axis_size("ctx")
    core = lax.rem(me, 2)
    wins = (win0, win1, win2, win3)

    chip, last = me // 2, count // 2 - 1
    even, odd = core == 0, core == 1
    prev, prev2, later = chip > 0, chip > 1, chip < last

    def at(step):
        return lax.rem(me + count + step, count)

    barrier = pltpu.get_barrier_semaphore()
    for step in (1, 2, 3, -1, -2, -3):
        @pl.when(me + step < count if step > 0 else me + step >= 0)
        def _():
            pl.semaphore_signal(barrier, inc=1, device_id=(at(step),), device_id_type=MESH)
    loads = [
        pltpu.make_async_copy(src, dst, load_sem.at[n])
        for n, (src, dst) in enumerate(
            (
                (k_hbm, k_ref), (v_hbm, v_ref), (parent_hbm, parent_ref),
                (start_hbm, start_ref), (q_hbm, q_ref), (o_hbm, o_ref),
            )
        )
    ]
    for copy in loads:
        copy.start()
    for copy in loads[:2]:
        copy.wait()

    def pack(h):
        lanes = slice(64 * h, 64 * h + 64)
        for b in range(BLOCKS):
            rows = slice(b * BLOCK, (b + 1) * BLOCK)
            wins[h][12 + b] = jnp.concatenate([k_ref[rows, lanes], v_ref[rows, lanes]], 1)
    pack(0)
    pl.semaphore_wait(barrier, jnp.minimum(me, 3) + jnp.minimum(count - 1 - me, 3))

    def fwd(h, part, src, dst, send, recv, step):
        size = BLOCKS // FWD_PARTS[h]
        return pltpu.make_async_remote_copy(
            src_ref=wins[h].at[pl.ds(src + part * size, size)],
            dst_ref=wins[h].at[pl.ds(dst + part * size, size)],
            send_sem=fwd_send.at[h, send, part], recv_sem=fwd_recv.at[h, recv, part],
            device_id=(at(step),), device_id_type=MESH,
        )

    def own_far(h, part):
        return fwd(h, part, OWN, FAR, 1, 2, 3)

    def own_near(h, part):
        return fwd(h, part, OWN, NEAR, 0, 0, 1)

    def near_far(h, part):
        return fwd(h, part, NEAR, FAR, 3, 2, 2)

    def near_mid(h, part):
        return fwd(h, part, NEAR, MID, 2, 1, 1)

    def far_mid(h, part):
        return fwd(h, part, FAR, MID, 2, 1, -1)

    def send_own(h, far=True, near=True):
        if far:
            @pl.when(even & later)
            def _():
                for part in range(FWD_PARTS[h]):
                    own_far(h, part).start()
        if near:
            @pl.when(even | later)
            def _():
                for part in range(FWD_PARTS[h]):
                    own_near(h, part).start()

    def relay(h):
        @pl.when(even & prev)
        def _():
            for part in range(FWD_PARTS[h]):
                own_near(h, part).wait_recv()

                @pl.when(later)
                def _():
                    near_far(h, part).start()
                near_mid(h, part).start()

        @pl.when(odd & prev)
        def _():
            for part in range(FWD_PARTS[h]):
                own_far(h, part).wait_recv()
                far_mid(h, part).start()

    def ready(h):
        for part in range(FWD_PARTS[h]):
            @pl.when(odd)
            def _():
                own_near(h, part).wait_recv()

            @pl.when(prev)
            def _():
                near_mid(h, part).wait_recv()

            @pl.when(even & prev2)
            def _():
                near_far(h, part).wait_recv()

    def back(h, part, src, dst, step):
        size = ROWS // BACK_PARTS[h]
        rows = pl.ds(part * size, size)
        return pltpu.make_async_remote_copy(
            src_ref=out_buf.at[h, src, rows], dst_ref=in_buf.at[h, dst, rows],
            send_sem=back_send.at[h, src, part], recv_sem=back_recv.at[h, dst, part],
            device_id=(at(step),), device_id_type=MESH,
        )

    def window_sum(h, distance, w):
        total = None
        for b in range(BLOCKS):
            if distance == 0 and w >= b:
                continue
            hit = jnp.where(slots[b] == (3 - distance) * BLOCKS + w, 1.0, 0.0)
            term = far_ref[h, b * BLOCK : (b + 1) * BLOCK, :] * hit
            total = term if total is None else total + term
        return total

    def block_rows(w):
        return slice(w * BLOCK, (w + 1) * BLOCK)

    def send(h, src, dst, step, distance, arrived):
        size = BLOCKS // BACK_PARTS[h]
        for part in range(BACK_PARTS[h]):
            for other in arrived:
                back(h, part, 0, other, 1).wait_recv()
            for w in range(part * size, (part + 1) * size):
                total = window_sum(h, distance, w)
                for other in arrived:
                    total = total + in_buf[h, other, block_rows(w), :].astype(F32)
                out_buf[h, src, block_rows(w), :] = total.astype(BF16)
            back(h, part, src, dst, step).start()

    def give(h):
        @pl.when(even & prev2)
        def _():
            send(h, 0, 1, -2, 3, ())

        @pl.when(even & prev)
        def _():
            send(h, 1, 0, 1, 2, ())

        @pl.when(odd & prev)
        def _():
            send(h, 0, 0, -1, 2, ())

        @pl.when(odd)
        def _():
            send(h, 1, 2, -1, 1, ())

    def merge_even(h):
        @pl.when(even & prev & later)
        def _():
            send(h, 2, 2, -1, 1, (0, 1))

        @pl.when(even & prev & (chip == last))
        def _():
            send(h, 2, 2, -1, 1, (0,))

    def merge_odd(h):
        @pl.when(odd & prev)
        def _():
            send(h, 2, 3, -3, 3, (0,))

    def take(h):
        for w in range(BLOCKS - 1):
            own_ref[h, block_rows(w), :] += window_sum(h, 0, w)

        @pl.when(even & later)
        def _():
            for part in range(BACK_PARTS[h]):
                back(h, part, 2, 3, -3).wait_recv()
            own_ref[h] += in_buf[h, 3].astype(F32)

        @pl.when(even | later)
        def _():
            for part in range(BACK_PARTS[h]):
                back(h, part, 1, 2, -1).wait_recv()
            own_ref[h] += in_buf[h, 2].astype(F32)

    send_own(0)
    pack(1)
    send_own(1)
    pack(2)
    pack(3)
    for copy in loads[2:]:
        copy.wait()
    first = me * BLOCKS
    oldest = jnp.maximum(3 * BLOCKS - first, 0)
    parents = [parent_ref[first + b] for b in range(BLOCKS)]
    slots = [
        jnp.where(p >= 0, jnp.clip(p - (first - 3 * BLOCKS), 0, 4 * BLOCKS - 1), -1)
        for p in parents
    ]
    for b in range(BLOCKS):
        s = start_ref[first + b]
        s2 = start_ref[jnp.maximum(parents[b], 0)]
        jj, ii = iota((BLOCK, BLOCK), 0), iota((BLOCK, BLOCK), 1)
        upto = jnp.where(s == 0, BLOCK, s)
        from_key = jnp.where(parents[b] >= 0, s2, BLOCK)
        own = jnp.where((jj >= s) == (ii >= s), 0.0, -1e30)
        far = jnp.where((ii < upto) & (jj >= from_key), 0.0, -1e30)
        bias_ref[b] = jnp.where(jj <= ii, own, far)
    relay(0)
    send_own(2, near=False)
    relay(1)
    send_own(2, far=False)
    send_own(3)
    for h in range(HEADS):
        ready(h)
        if h == 2:
            merge_even(0)
        if h == 3:
            merge_odd(2)
        for b in range(BLOCKS):
            slot = jnp.maximum(parent_ref[first + b] - (first - 3 * BLOCKS), oldest)
            compute_block(
                h, b, wins[h][12 + b], wins[h][slot], q_ref, o_ref, dq_ref, bias_ref, own_ref, far_ref
            )
        if h in (1, 2):
            merge_odd(h - 1)
        if h < 2:
            relay(h + 2)
        give(h)
        if h == 2:
            merge_even(1)
    merge_odd(3)
    merge_even(2)
    take(0)
    take(1)
    merge_even(3)
    take(2)
    take(3)
    for h in range(0, HEADS, 2):
        lanes = slice(64 * h, 64 * h + 128)
        a, b = own_ref[h], own_ref[h + 1]
        dk_ref[:, lanes] = jnp.concatenate([a[:, :64], b[:, :64]], 1).astype(BF16)
        dv_ref[:, lanes] = jnp.concatenate([a[:, 64:], b[:, 64:]], 1).astype(BF16)
    for h in range(HEADS):
        for part in range(FWD_PARTS[h]):
            @pl.when(even | later)
            def _():
                own_near(h, part).wait_send()

            @pl.when(even & later)
            def _():
                own_far(h, part).wait_send()

            @pl.when(prev)
            def _():
                near_mid(h, part).wait_send()

            @pl.when(even & prev & later)
            def _():
                near_far(h, part).wait_send()
        for part in range(BACK_PARTS[h]):
            @pl.when(odd | prev)
            def _():
                back(h, part, 1, 0, 1).wait_send()

            @pl.when((odd & prev) | prev2)
            def _():
                back(h, part, 0, 0, 1).wait_send()

            @pl.when(prev)
            def _():
                back(h, part, 2, 0, 1).wait_send()


def write_out(dq_in, dk_in, dv_in, dq_out, dk_out, dv_out, sem):
    copies = [
        pltpu.make_async_copy(src, dst, sem.at[n])
        for n, (src, dst) in enumerate(((dq_in, dq_out), (dk_in, dk_out), (dv_in, dv_out)))
    ]
    for copy in copies:
        copy.start()
    for copy in copies:
        copy.wait()


def shards(q, k, v, o, parent_block, seg_start):
    hbm = pl.BlockSpec(memory_space=pltpu.HBM)
    vmem = pl.BlockSpec(memory_space=pltpu.VMEM)
    width = q.shape[1]
    results = pl.pallas_call(
        kernel,
        out_shape=(
            jax.ShapeDtypeStruct(q.shape, BF16),
            jax.ShapeDtypeStruct(k.shape, BF16),
            jax.ShapeDtypeStruct(v.shape, BF16),
        ),
        in_specs=[hbm] * 6,
        out_specs=(vmem,) * 3,
        scratch_shapes=[
            pltpu.VMEM(k.shape, BF16),
            pltpu.VMEM(v.shape, BF16),
            pltpu.SMEM(parent_block.shape, jnp.int32),
            pltpu.SMEM(seg_start.shape, jnp.int32),
            pltpu.VMEM((ROWS, width), BF16),
            pltpu.VMEM((ROWS, width), BF16),
        ]
        + [pltpu.VMEM((4 * BLOCKS, BLOCK, BLOCK), BF16)] * HEADS
        + [
            pltpu.VMEM((HEADS, ROWS, BLOCK), F32),
            pltpu.VMEM((HEADS, ROWS, BLOCK), F32),
            pltpu.VMEM((BLOCKS, BLOCK, BLOCK), F32),
            pltpu.VMEM((HEADS, 3, ROWS, BLOCK), BF16),
            pltpu.VMEM((HEADS, 4, ROWS, BLOCK), BF16),
            pltpu.SemaphoreType.DMA((6,)),
            pltpu.SemaphoreType.DMA((HEADS, 4, 4)),
            pltpu.SemaphoreType.DMA((HEADS, 3, 4)),
            pltpu.SemaphoreType.DMA((HEADS, 3, 4)),
            pltpu.SemaphoreType.DMA((HEADS, 4, 4)),
        ],
        compiler_params=pltpu.CompilerParams(
            collective_id=0, has_side_effects=True, vmem_limit_bytes=48 * 2**20
        ),
    )(*(pltpu.with_memory_space_constraint(x, pltpu.HBM) for x in (q, o, k, v, parent_block, seg_start)))
    return pl.pallas_call(
        write_out,
        out_shape=tuple(jax.ShapeDtypeStruct(x.shape, x.dtype) for x in results),
        in_specs=[pl.BlockSpec(memory_space=pl.ANY)] * 3,
        out_specs=(hbm,) * 3,
        scratch_shapes=[pltpu.SemaphoreType.DMA((3,))],
        compiler_params=pltpu.CompilerParams(vmem_limit_bytes=2**20),
    )(*results)


def solution(mesh):
    rows = P("ctx", None)
    return jax.shard_map(
        shards,
        mesh=mesh,
        in_specs=(rows, rows, rows, rows, P(), P()),
        out_specs=(rows, rows, rows),
        check_vma=False,
    )
```

```python
import jax
import jax.numpy as jnp
from jax import lax
from jax.experimental import pallas as pl
from jax.experimental.pallas import tpu as pltpu
from jax.sharding import PartitionSpec as P

HEADS = 4
BLOCK = 128
BLOCKS = 4
ROWS = BLOCK * BLOCKS
F32, BF16 = jnp.float32, jnp.bfloat16
SCALE = 0.125
EXP2_SCALE = SCALE * 1.4426950408889634
NT = (((1,), (1,)), ((), ()))
NN = (((1,), (0,)), ((), ()))
TN = (((0,), (0,)), ((), ()))
MESH = pl.DeviceIdType.MESH
OWN, NEAR, MID, FAR = 12, 8, 4, 0
FWD_PARTS = (4, 1, 1, 1)
BACK_PARTS = (1, 1, 1, 4)


def dot(a, b, dims):
    return lax.dot_general(a, b, dims, preferred_element_type=F32)


def iota(shape, dim):
    return lax.broadcasted_iota(jnp.int32, shape, dim)


def swap_halves(x):
    return jnp.concatenate([x[:, 64:], x[:, :64]], 1)


def compute_block(h, b, own_kv, far_kv, q_ref, o_ref, dq_ref, bias_ref, own_ref, far_ref):
    rows = slice(b * BLOCK, (b + 1) * BLOCK)
    kv = jnp.concatenate([own_kv, far_kv], 0)
    vk = swap_halves(kv)
    low = iota((256, 128), 1) < 64
    zero = jnp.zeros_like(kv)
    keys = jnp.concatenate([jnp.where(low, kv, zero), jnp.where(low, zero, vk)], 0)
    values = jnp.concatenate([jnp.where(low, vk, zero), jnp.where(low, zero, kv)], 0)
    bias = bias_ref[b]
    bias = jnp.concatenate([bias, bias], 1)
    causal = iota((BLOCK, 256), 0) <= lax.rem(iota((BLOCK, 256), 1), BLOCK)
    causal_low = causal.astype(F32).astype(BF16)
    queries, grads, scores = [], [], []
    for quad in range(2):
        c = h * 512 + quad * 256
        qs = jnp.concatenate([q_ref[rows, c : c + 128], q_ref[rows, c + 128 : c + 256]], 0)
        os = jnp.concatenate([o_ref[rows, c : c + 128], o_ref[rows, c + 128 : c + 256]], 0)
        queries.append(qs)
        grads.append(os)
        scores.append((dot(keys, qs, NT), dot(values, os, NT)))
    g_parts, p_parts = ([], []), ([], [])
    for quad in range(2):
        c = h * 512 + quad * 256
        s_all, d_all = scores[quad]
        dq_t = []
        for odd in range(2):
            r = odd * 256
            s = jnp.where(causal, s_all[r : r + 128], s_all[r + 128 : r + 256]) + bias
            w = jnp.exp2((s - jnp.max(s, 0, keepdims=True)) * EXP2_SCALE)
            inv = 1.0 / jnp.sum(w, 0, keepdims=True)
            d = jnp.where(causal, d_all[r : r + 128], d_all[r + 128 : r + 256])
            delta = jnp.sum(w * d, 0, keepdims=True) * inv
            p = w * inv
            g = (p * (d - delta)).astype(BF16)
            p = p.astype(BF16)
            p_own, g_own = p * causal_low, g * causal_low
            p = jnp.concatenate([p_own, p - p_own], 0)
            g = jnp.concatenate([g_own, g - g_own], 0)
            p_parts[odd].append(p)
            g_parts[odd].append(g)
            dq_t.append(dot(kv[:, :64], g, TN))
        dq = jnp.concatenate(dq_t, 0) * SCALE
        dq_ref[rows, c : c + 128] = dq[:, :128].T.astype(BF16)
        dq_ref[rows, c + 128 : c + 256] = dq[:, 128:].T.astype(BF16)
    qs, os = jnp.concatenate(queries, 0), jnp.concatenate(grads, 0)
    k_even = dot(jnp.concatenate(g_parts[0], 1), qs, NN) * SCALE
    k_odd = dot(jnp.concatenate(g_parts[1], 1), qs, NN) * SCALE
    v_even = dot(jnp.concatenate(p_parts[0], 1), os, NN)
    v_odd = dot(jnp.concatenate(p_parts[1], 1), os, NN)
    out = jnp.where(low, k_even, v_odd) + swap_halves(jnp.where(low, v_even, k_odd))
    own_ref[h, rows, :] = out[:BLOCK]
    far_ref[h, rows, :] = out[BLOCK:]


def kernel(
    q_hbm, o_hbm, k_hbm, v_hbm, parent_hbm, start_hbm, dq_ref, dk_ref, dv_ref,
    k_ref, v_ref, parent_ref, start_ref, q_ref, o_ref, win0, win1, win2, win3, own_ref, far_ref, bias_ref, out_buf, in_buf,
    load_sem, fwd_send, fwd_recv, back_send, back_recv,
):
    me = lax.axis_index("ctx")
    count = lax.axis_size("ctx")
    core = lax.rem(me, 2)
    wins = (win0, win1, win2, win3)

    chip, last = me // 2, count // 2 - 1
    even, odd = core == 0, core == 1
    prev, prev2, later = chip > 0, chip > 1, chip < last

    def at(step):
        return lax.rem(me + count + step, count)

    barrier = pltpu.get_barrier_semaphore()
    for step in (1, 2, 3, -1, -2, -3):
        @pl.when(me + step < count if step > 0 else me + step >= 0)
        def _():
            pl.semaphore_signal(barrier, inc=1, device_id=(at(step),), device_id_type=MESH)
    loads = [
        pltpu.make_async_copy(src, dst, load_sem.at[n])
        for n, (src, dst) in enumerate(
            (
                (k_hbm, k_ref), (v_hbm, v_ref), (parent_hbm, parent_ref),
                (start_hbm, start_ref), (q_hbm, q_ref), (o_hbm, o_ref),
            )
        )
    ]
    for copy in loads:
        copy.start()
    for copy in loads[:2]:
        copy.wait()

    def pack(h):
        lanes = slice(64 * h, 64 * h + 64)
        for b in range(BLOCKS):
            rows = slice(b * BLOCK, (b + 1) * BLOCK)
            wins[h][12 + b] = jnp.concatenate([k_ref[rows, lanes], v_ref[rows, lanes]], 1)
    pack(0)
    pl.semaphore_wait(barrier, jnp.minimum(me, 3) + jnp.minimum(count - 1 - me, 3))

    def fwd(h, part, src, dst, send, recv, step):
        size = BLOCKS // FWD_PARTS[h]
        return pltpu.make_async_remote_copy(
            src_ref=wins[h].at[pl.ds(src + part * size, size)],
            dst_ref=wins[h].at[pl.ds(dst + part * size, size)],
            send_sem=fwd_send.at[h, send, part], recv_sem=fwd_recv.at[h, recv, part],
            device_id=(at(step),), device_id_type=MESH,
        )

    def own_far(h, part):
        return fwd(h, part, OWN, FAR, 1, 2, 3)

    def own_near(h, part):
        return fwd(h, part, OWN, NEAR, 0, 0, 1)

    def near_far(h, part):
        return fwd(h, part, NEAR, FAR, 3, 2, 2)

    def near_mid(h, part):
        return fwd(h, part, NEAR, MID, 2, 1, 1)

    def far_mid(h, part):
        return fwd(h, part, FAR, MID, 2, 1, -1)

    def send_own(h, far=True, near=True):
        if far:
            @pl.when(even & later)
            def _():
                for part in range(FWD_PARTS[h]):
                    own_far(h, part).start()
        if near:
            @pl.when(even | later)
            def _():
                for part in range(FWD_PARTS[h]):
                    own_near(h, part).start()

    def relay(h):
        @pl.when(even & prev)
        def _():
            for part in range(FWD_PARTS[h]):
                own_near(h, part).wait_recv()

                @pl.when(later)
                def _():
                    near_far(h, part).start()
                near_mid(h, part).start()

        @pl.when(odd & prev)
        def _():
            for part in range(FWD_PARTS[h]):
                own_far(h, part).wait_recv()
                far_mid(h, part).start()

    def ready(h):
        for part in range(FWD_PARTS[h]):
            @pl.when(odd)
            def _():
                own_near(h, part).wait_recv()

            @pl.when(prev)
            def _():
                near_mid(h, part).wait_recv()

            @pl.when(even & prev2)
            def _():
                near_far(h, part).wait_recv()

    def back(h, part, src, dst, step):
        size = ROWS // BACK_PARTS[h]
        rows = pl.ds(part * size, size)
        return pltpu.make_async_remote_copy(
            src_ref=out_buf.at[h, src, rows], dst_ref=in_buf.at[h, dst, rows],
            send_sem=back_send.at[h, src, part], recv_sem=back_recv.at[h, dst, part],
            device_id=(at(step),), device_id_type=MESH,
        )

    def window_sum(h, distance, w):
        total = None
        for b in range(BLOCKS):
            if distance == 0 and w >= b:
                continue
            hit = jnp.where(slots[b] == (3 - distance) * BLOCKS + w, 1.0, 0.0)
            term = far_ref[h, b * BLOCK : (b + 1) * BLOCK, :] * hit
            total = term if total is None else total + term
        return total

    def block_rows(w):
        return slice(w * BLOCK, (w + 1) * BLOCK)

    def send(h, src, dst, step, distance, arrived):
        size = BLOCKS // BACK_PARTS[h]
        for part in range(BACK_PARTS[h]):
            for other in arrived:
                back(h, part, 0, other, 1).wait_recv()
            for w in range(part * size, (part + 1) * size):
                total = window_sum(h, distance, w)
                for other in arrived:
                    total = total + in_buf[h, other, block_rows(w), :].astype(F32)
                out_buf[h, src, block_rows(w), :] = total.astype(BF16)
            back(h, part, src, dst, step).start()

    def give(h):
        @pl.when(even & prev2)
        def _():
            send(h, 0, 1, -2, 3, ())

        @pl.when(even & prev)
        def _():
            send(h, 1, 0, 1, 2, ())

        @pl.when(odd & prev)
        def _():
            send(h, 0, 0, -1, 2, ())

        @pl.when(odd)
        def _():
            send(h, 1, 2, -1, 1, ())

    def merge_even(h):
        @pl.when(even & prev & later)
        def _():
            send(h, 2, 2, -1, 1, (0, 1))

        @pl.when(even & prev & (chip == last))
        def _():
            send(h, 2, 2, -1, 1, (0,))

    def merge_odd(h):
        @pl.when(odd & prev)
        def _():
            send(h, 2, 3, -3, 3, (0,))

    def take(h):
        for w in range(BLOCKS - 1):
            own_ref[h, block_rows(w), :] += window_sum(h, 0, w)

        @pl.when(even & later)
        def _():
            for part in range(BACK_PARTS[h]):
                back(h, part, 2, 3, -3).wait_recv()
            own_ref[h] += in_buf[h, 3].astype(F32)

        @pl.when(even | later)
        def _():
            for part in range(BACK_PARTS[h]):
                back(h, part, 1, 2, -1).wait_recv()
            own_ref[h] += in_buf[h, 2].astype(F32)

    send_own(0)
    pack(1)
    send_own(1)
    pack(2)
    pack(3)
    for copy in loads[2:]:
        copy.wait()
    first = me * BLOCKS
    oldest = jnp.maximum(3 * BLOCKS - first, 0)
    parents = [parent_ref[first + b] for b in range(BLOCKS)]
    slots = [
        jnp.where(p >= 0, jnp.clip(p - (first - 3 * BLOCKS), 0, 4 * BLOCKS - 1), -1)
        for p in parents
    ]
    for b in range(BLOCKS):
        s = start_ref[first + b]
        s2 = start_ref[jnp.maximum(parents[b], 0)]
        jj, ii = iota((BLOCK, BLOCK), 0), iota((BLOCK, BLOCK), 1)
        upto = jnp.where(s == 0, BLOCK, s)
        from_key = jnp.where(parents[b] >= 0, s2, BLOCK)
        own = jnp.where((jj >= s) == (ii >= s), 0.0, -1e30)
        far = jnp.where((ii < upto) & (jj >= from_key), 0.0, -1e30)
        bias_ref[b] = jnp.where(jj <= ii, own, far)
    relay(0)
    send_own(2, near=False)
    relay(1)
    send_own(2, far=False)
    for h in range(HEADS):
        ready(h)
        if h == 2:
            merge_even(0)
        if h == 3:
            merge_odd(2)
        for b in range(BLOCKS):
            slot = jnp.maximum(parent_ref[first + b] - (first - 3 * BLOCKS), oldest)
            compute_block(
                h, b, wins[h][12 + b], wins[h][slot], q_ref, o_ref, dq_ref, bias_ref, own_ref, far_ref
            )
        if h in (1, 2):
            merge_odd(h - 1)
        if h == 0:
            send_own(3)
        if h < 2:
            relay(h + 2)
        give(h)
        if h == 2:
            merge_even(1)
    def finish(h):
        lanes = slice(64 * h, 64 * h + 128)
        a, b = own_ref[h], own_ref[h + 1]
        dk_ref[:, lanes] = jnp.concatenate([a[:, :64], b[:, :64]], 1).astype(BF16)
        dv_ref[:, lanes] = jnp.concatenate([a[:, 64:], b[:, 64:]], 1).astype(BF16)

    merge_odd(3)
    merge_even(2)
    take(0)
    take(1)
    merge_even(3)
    finish(0)
    take(2)
    take(3)
    finish(2)
    for h in range(HEADS):
        for part in range(FWD_PARTS[h]):
            @pl.when(even | later)
            def _():
                own_near(h, part).wait_send()

            @pl.when(even & later)
            def _():
                own_far(h, part).wait_send()

            @pl.when(prev)
            def _():
                near_mid(h, part).wait_send()

            @pl.when(even & prev & later)
            def _():
                near_far(h, part).wait_send()
        for part in range(BACK_PARTS[h]):
            @pl.when(odd | prev)
            def _():
                back(h, part, 1, 0, 1).wait_send()

            @pl.when((odd & prev) | prev2)
            def _():
                back(h, part, 0, 0, 1).wait_send()

            @pl.when(prev)
            def _():
                back(h, part, 2, 0, 1).wait_send()


def write_out(dq_in, dk_in, dv_in, dq_out, dk_out, dv_out, sem):
    copies = [
        pltpu.make_async_copy(src, dst, sem.at[n])
        for n, (src, dst) in enumerate(((dq_in, dq_out), (dk_in, dk_out), (dv_in, dv_out)))
    ]
    for copy in copies:
        copy.start()
    for copy in copies:
        copy.wait()


def shards(q, k, v, o, parent_block, seg_start):
    hbm = pl.BlockSpec(memory_space=pltpu.HBM)
    vmem = pl.BlockSpec(memory_space=pltpu.VMEM)
    width = q.shape[1]
    results = pl.pallas_call(
        kernel,
        out_shape=(
            jax.ShapeDtypeStruct(q.shape, BF16),
            jax.ShapeDtypeStruct(k.shape, BF16),
            jax.ShapeDtypeStruct(v.shape, BF16),
        ),
        in_specs=[hbm] * 6,
        out_specs=(vmem,) * 3,
        scratch_shapes=[
            pltpu.VMEM(k.shape, BF16),
            pltpu.VMEM(v.shape, BF16),
            pltpu.SMEM(parent_block.shape, jnp.int32),
            pltpu.SMEM(seg_start.shape, jnp.int32),
            pltpu.VMEM((ROWS, width), BF16),
            pltpu.VMEM((ROWS, width), BF16),
        ]
        + [pltpu.VMEM((4 * BLOCKS, BLOCK, BLOCK), BF16)] * HEADS
        + [
            pltpu.VMEM((HEADS, ROWS, BLOCK), F32),
            pltpu.VMEM((HEADS, ROWS, BLOCK), F32),
            pltpu.VMEM((BLOCKS, BLOCK, BLOCK), F32),
            pltpu.VMEM((HEADS, 3, ROWS, BLOCK), BF16),
            pltpu.VMEM((HEADS, 4, ROWS, BLOCK), BF16),
            pltpu.SemaphoreType.DMA((6,)),
            pltpu.SemaphoreType.DMA((HEADS, 4, 4)),
            pltpu.SemaphoreType.DMA((HEADS, 3, 4)),
            pltpu.SemaphoreType.DMA((HEADS, 3, 4)),
            pltpu.SemaphoreType.DMA((HEADS, 4, 4)),
        ],
        compiler_params=pltpu.CompilerParams(
            collective_id=0, has_side_effects=True, vmem_limit_bytes=48 * 2**20
        ),
    )(*(pltpu.with_memory_space_constraint(x, pltpu.HBM) for x in (q, o, k, v, parent_block, seg_start)))
    return pl.pallas_call(
        write_out,
        out_shape=tuple(jax.ShapeDtypeStruct(x.shape, x.dtype) for x in results),
        in_specs=[pl.BlockSpec(memory_space=pl.ANY)] * 3,
        out_specs=(hbm,) * 3,
        scratch_shapes=[pltpu.SemaphoreType.DMA((3,))],
        compiler_params=pltpu.CompilerParams(vmem_limit_bytes=2**20),
    )(*results)


def solution(mesh):
    rows = P("ctx", None)
    return jax.shard_map(
        shards,
        mesh=mesh,
        in_specs=(rows, rows, rows, rows, P(), P()),
        out_specs=(rows, rows, rows),
        check_vma=False,
    )
```
